128 devices in a mesh: gx: 16 (over x_lo, z, core), gy: 8 (over x_hi, y).
Axes of the slice: x: 4 (x_hi: 2, x_lo: 2; x = x_hi * 2 + x_lo), y: 4, z: 4, core: 2. Of those that a mesh axis runs over, the one named last changes fastest.
Arguments:
- basin_velocity: float32 [3, 16, 1024, 1024], P(None, None, 'gx', 'gy'), may hold values from -6 to 6
- basin_stress: float32 [6, 16, 1024, 1024], P(None, None, 'gx', 'gy'), may hold values from -6 to 6
- basin_media: float32 [3, 16, 1024, 1024], P(None, None, 'gx', 'gy'), may hold values from 0.5 to 2
- box_velocity: float32 [3, 8, 1024, 1024], P(None, None, 'gx', 'gy'), may hold values from -6 to 6
- box_stress: float32 [6, 8, 1024, 1024], P(None, None, 'gx', 'gy'), may hold values from -6 to 6
- zone_ids: int32 [8, 1024, 1024], P(None, 'gx', 'gy'), may hold values from 0 to 7
- zone_media: float32 [3, 8], replicated, may hold values from 0.5 to 2
- corridor_tile: int32 [16, 8, 8192, 1], P('gx'), may hold values from 0 to 7; in each aligned block of 8192 rows (0 to 8191, 8192 to 16383, ..., all dimensions but the last counted through in order) at most 2048 rows name the same one
- corridor_cell: int32 [16, 8, 8192], P('gx'), may hold values from 0 to 8191
- drm_stiff: float32 [16, 8, 64, 128, 128], P('gx', 'gy'), may hold values from -0.5 to 0.5
- drm_mass: float32 [16, 8, 64, 128, 128], P('gx', 'gy'), may hold values from -0.5 to 0.5
Outputs:
- basin_velocity_next: float32 [3, 16, 1024, 1024], P(None, None, 'gx', 'gy')
- basin_stress_next: float32 [6, 16, 1024, 1024], P(None, None, 'gx', 'gy')
- box_velocity_next: float32 [3, 8, 1024, 1024], P(None, None, 'gx', 'gy')
- box_stress_next: float32 [6, 8, 1024, 1024], P(None, None, 'gx', 'gy')
The draws below stay inside these ranges and needn't reach their ends.
Inputs may be any that keep to these rules, and one draw needn't show every extreme that they name: `corridor_tile`: within the 8192 rows of one owner (one index pair of the first two dimensions) no tile is named by more than 2048 rows, and in every draw some owner has a tile named by exactly 2048 rows.
All inputs are finite; a program needn't handle non-finite values.
Results may differ from the reference program's by a relative error of at most 0.0001.
Values sent between devices are 32-bit elements; how exact they have to be, the bound alone decides.
No kernel may reach another device: no remote copies, remote signals or barrier semaphores. Data moves between devices by JAX's collectives and lax.ppermute only.
A program may use at most 128 MiB of HBM per device.

```python
import math
import jax
import jax.numpy as jnp
import numpy as np
from jax import lax

NZ = 16
BZ = 8
CX = 64
CY = 128
STEPS = 2
ZR = 8
ZONES = 8
BLK = 128
TX = 16
TY = 8
NX = 1024
NY = 1024
RD = 8192
CAP = 2048
GROUPS = 64


def touch_ends(values, stream_key, low, top_value):
    longest = values.shape.index(max(values.shape))
    spots = []
    for shift in (0, 1):
        where = [jax.random.randint(jax.random.fold_in(stream_key, axis), (), 0, length) for axis, length in enumerate(values.shape)]
        where[longest] = (where[longest] + shift) % values.shape[longest]
        spots.append(tuple(where))
    return values.at[spots[0]].set(low).at[spots[1]].set(top_value)


def block_scale(rng, extent, cuts, least, largest):
    def one(axis_at, parts):
        draws = jax.random.uniform(jax.random.fold_in(jax.random.fold_in(rng, 6), axis_at), (parts,), jnp.float32, least / len(cuts), largest / len(cuts))
        return jnp.repeat(jnp.exp(draws), extent[axis_at] // parts).reshape((-1,) + (1,) * (len(extent) - axis_at - 1))

    factor_of = one(*cuts[0])
    for cut in cuts[1:]:
        factor_of = factor_of * one(*cut)
    return factor_of


def deal_out(rng, own, number, rows, count, top, limit, skew):
    ranking = jax.random.permutation(rng, count)
    crowded, usual = load_shares(count, rows * top, limit, skew, True), load_shares(count, rows * top, limit, skew, False)
    places = jnp.arange(count)

    def named(lengths, turn):
        used = int((lengths > 0).sum())
        fixed = max(1, used // 4)
        shifted = fixed + (places - fixed + turn * (used - fixed)) % max(1, count - fixed)
        return jnp.zeros((count,), jnp.int32).at[ranking[jnp.where(places < fixed, places, shifted)]].set(jnp.asarray(lengths, jnp.int32))

    lengths = jnp.where(number % 4 == 0, named(crowded, number // 4), named(usual, number - number // 4 - 1))
    mixed = jax.random.permutation(jax.random.fold_in(own, 3), count)
    source_of, receiver = mixed[0:count // 2 * 2:2], mixed[1:count // 2 * 2:2]
    slack = jnp.minimum(lengths[source_of] - 1, limit - lengths[receiver]) // 2
    slack = jnp.where((source_of == ranking[0]) | (receiver == ranking[0]) | (lengths[receiver] == 0), 0, jnp.maximum(slack, 0))
    shifted = jax.random.randint(jax.random.fold_in(own, 4), (count // 2,), 0, 1 << 20) % (slack + 1)
    lengths = lengths.at[source_of].add(-shifted).at[receiver].add(shifted)
    labels = jnp.searchsorted(jnp.cumsum(lengths), jnp.arange(rows * top), side="right").astype(jnp.int32)
    listing = labels.reshape(top, rows).T
    listing = listing[jax.random.permutation(jax.random.fold_in(own, 1), rows)]
    turn = jax.random.randint(jax.random.fold_in(own, 2), (rows, 1), 0, top)
    return jnp.take_along_axis(listing, (jnp.arange(top)[None, :] + turn) % top, axis=1)


def load_shares(count, total, most, slope, full):
    loads = [(1 << 20) // math.isqrt(standing ** slope) + 1 for standing in range(1, count + 1)]
    largest = most if full else min(most, max(-(-total // count), total * loads[0] // sum(loads)))
    least = 1 if total - largest >= count - 1 else 0
    counts, spare = [largest] + [least] * (count - 1), total - largest - least * (count - 1)
    while spare > 0:
        free = [i for i in range(1, count) if counts[i] < largest] or [i for i in range(1, count) if counts[i] < most]
        pool, budget = sum([loads[i] for i in free]), spare
        for i in free:
            extra = min(most - counts[i], max(1, budget * loads[i] // pool), spare)
            counts[i] = counts[i] + extra
            spare = spare - extra
    return np.array(counts)


def gaussian(stream_key, extent, width, most, shards=(), kind=jnp.bfloat16):
    loudness = block_scale(stream_key, extent, shards, -0.22, 0.18) if shards else 1.0
    entries = jax.random.normal(stream_key, extent, jnp.float32) * width * loudness
    return jnp.minimum(jnp.maximum(entries, -most), most).astype(kind)


def setup_inputs(seed: int = 0) -> dict:
    key_list = jax.random.split(jax.random.key(seed), 12)
    basin_velocity = gaussian(key_list[0], (3, NZ, NX, NY), 1.0, 6.0, ((2, 16), (3, 8)), jnp.float32)
    basin_stress = gaussian(key_list[1], (6, NZ, NX, NY), 1.0, 6.0, ((2, 16), (3, 8)), jnp.float32)
    basin_media = jnp.clip(jnp.exp(math.log(2.0) - 1.3862944 * jax.random.uniform(key_list[2], (3, NZ, NX, NY), jnp.float32) ** block_scale(key_list[2], (3, NZ, NX, NY), ((2, 16), (3, 8)), -0.2, 0.2)), 0.5, 2.0)
    box_velocity = gaussian(key_list[3], (3, BZ, NX, NY), 1.0, 6.0, ((2, 16), (3, 8)), jnp.float32)
    box_stress = gaussian(key_list[4], (6, BZ, NX, NY), 1.0, 6.0, ((2, 16), (3, 8)), jnp.float32)
    zone_ids = touch_ends(jax.random.randint(key_list[5], (BZ, NX, NY), 0, ZONES), jax.random.fold_in(key_list[5], 1), 0, ZONES - 1).astype(jnp.int32)
    zone_media = jnp.clip(jnp.exp(jax.random.uniform(key_list[6], (3, ZONES), jnp.float32, math.log(0.5), math.log(2.0))), 0.5, 2.0)
    corridor_tile_keys = jax.random.split(jax.random.fold_in(key_list[7], 1), TX * TY * RD // RD)
    corridor_tile_turns = jax.random.permutation(jax.random.fold_in(key_list[7], 3), TX * TY * RD // RD)
    corridor_tile = jax.vmap(lambda own, number: deal_out(jax.random.fold_in(key_list[7], 2), own, number, RD, TY, 1, CAP, 2))(corridor_tile_keys, corridor_tile_turns).reshape((TX, TY, RD, 1))
    corridor_cell = touch_ends(jax.random.randint(key_list[8], (TX, TY, RD), 0, CX * CY), jax.random.fold_in(key_list[8], 1), 0, (CX * CY) - 1).astype(jnp.int32)
    drm_stiff = gaussian(key_list[9], (TX, TY, GROUPS, BLK, BLK), BLK ** -0.5, 0.5, ((0, 16), (1, 8)), jnp.float32)
    drm_mass = gaussian(key_list[10], (TX, TY, GROUPS, BLK, BLK), BLK ** -0.5, 0.5, ((0, 16), (1, 8)), jnp.float32)
    return dict(basin_velocity=basin_velocity, basin_stress=basin_stress, basin_media=basin_media, box_velocity=box_velocity, box_stress=box_stress, zone_ids=zone_ids, zone_media=zone_media, corridor_tile=corridor_tile, corridor_cell=corridor_cell, drm_stiff=drm_stiff, drm_mass=drm_mass)


COURANT = 0.12
FOURTH_NEAR = 9.0 / 8.0
FOURTH_FAR = 1.0 / 24.0


def forward_diff(padded, dimension):
    length = padded.shape[dimension] - 4

    def window(offset):
        return lax.slice_in_dim(padded, offset, offset + length, axis=dimension)
    return FOURTH_NEAR * (window(3) - window(2)) - FOURTH_FAR * (window(4) - window(1))


def backward_diff(padded, dimension):
    length = padded.shape[dimension] - 4

    def window(offset):
        return lax.slice_in_dim(padded, offset, offset + length, axis=dimension)
    return FOURTH_NEAR * (window(2) - window(1)) - FOURTH_FAR * (window(3) - window(0))


def new_velocity(velocity, buoyancy, slopes):
    comp_x = velocity[0] + COURANT * buoyancy * (slopes[0] + slopes[1] + slopes[2])
    comp_y = velocity[1] + COURANT * buoyancy * (slopes[3] + slopes[4] + slopes[5])
    comp_z = velocity[2] + COURANT * buoyancy * (slopes[6] + slopes[7] + slopes[8])
    return jnp.stack([comp_x, comp_y, comp_z])


def new_stress(stress, material, slopes):
    lame_first = material[0]
    shear_mod = material[1]
    modulus = lame_first + 2.0 * shear_mod
    along_x, along_y, along_z = slopes[0], slopes[1], slopes[2]
    comp_xx = stress[0] + COURANT * (modulus * along_x + lame_first * (along_y + along_z))
    comp_xz = stress[1] + COURANT * shear_mod * (slopes[5] + slopes[6])
    comp_xy = stress[2] + COURANT * shear_mod * (slopes[3] + slopes[4])
    comp_yz = stress[3] + COURANT * shear_mod * (slopes[7] + slopes[8])
    comp_yy = stress[4] + COURANT * (modulus * along_y + lame_first * (along_x + along_z))
    comp_zz = stress[5] + COURANT * (modulus * along_z + lame_first * (along_x + along_y))
    return jnp.stack([comp_xx, comp_xz, comp_xy, comp_yz, comp_yy, comp_zz])


def spatial_derivative(values, dimension, forward):
    padded = jnp.pad(values, 2)
    crop_index = [slice(2, -2), slice(2, -2), slice(2, -2)]
    crop_index[dimension] = slice(None)
    cropped = padded[tuple(crop_index)]
    if forward:
        return forward_diff(cropped, dimension)
    return backward_diff(cropped, dimension)


def grid_velocity(velocity, stress, material):
    slopes = (spatial_derivative(stress[0], 1, True), spatial_derivative(stress[2], 2, False),
              spatial_derivative(stress[1], 0, False), spatial_derivative(stress[2], 1, False),
              spatial_derivative(stress[4], 2, True), spatial_derivative(stress[3], 0, False),
              spatial_derivative(stress[1], 1, False), spatial_derivative(stress[3], 2, False),
              spatial_derivative(stress[5], 0, True))
    return new_velocity(velocity, material[2], slopes)


def grid_stress(stress, velocity, material):
    slopes = (spatial_derivative(velocity[0], 1, False), spatial_derivative(velocity[1], 2, False),
              spatial_derivative(velocity[2], 0, False), spatial_derivative(velocity[0], 2, True),
              spatial_derivative(velocity[1], 1, True), spatial_derivative(velocity[0], 0, True),
              spatial_derivative(velocity[2], 1, True), spatial_derivative(velocity[1], 0, True),
              spatial_derivative(velocity[2], 2, True))
    return new_stress(stress, material, slopes)


def free_field(velocity, corridor_tile, corridor_cell):
    layer_values = velocity[:, ZR]
    tile_of_row = corridor_tile[..., 0]
    rows_x = (jnp.arange(TX, dtype=jnp.int32)[:, None, None] * CX + corridor_cell // CY).astype(jnp.int32)
    rows_y = (tile_of_row * CY + corridor_cell % CY).astype(jnp.int32)
    return layer_values[:, rows_x, rows_y]


def drm_forces(current, previous, drm_stiff, drm_mass):
    present = current.reshape(3, TX, TY, GROUPS, BLK)
    change = ((current - previous) / COURANT).reshape(3, TX, TY, GROUPS, BLK)
    stiff_part = jnp.einsum("ijgab,cijgb->cijga", drm_stiff, present, precision=lax.Precision.HIGHEST)
    mass_part = jnp.einsum("ijgab,cijgb->cijga", drm_mass, change, precision=lax.Precision.HIGHEST)
    summed = -(stiff_part + mass_part)
    summed = summed.reshape(3, TX, TY, CX, CY).transpose(0, 1, 3, 2, 4)
    return summed.reshape(3, TX * CX, TY * CY)


def reference(basin_velocity, basin_stress, basin_media, box_velocity, box_stress, zone_ids, zone_media, corridor_tile, corridor_cell, drm_stiff, drm_mass):
    box_media = zone_media[:, zone_ids]
    previous = free_field(basin_velocity, corridor_tile, corridor_cell)
    for number in range(STEPS):
        basin_velocity = grid_velocity(basin_velocity, basin_stress, basin_media)
        box_velocity = grid_velocity(box_velocity, box_stress, box_media)
        current = free_field(basin_velocity, corridor_tile, corridor_cell)
        forces = drm_forces(current, previous, drm_stiff, drm_mass)
        previous = current
        box_velocity = box_velocity.at[:, BZ - 1].add(COURANT * box_media[2, BZ - 1] * forces)
        basin_stress = grid_stress(basin_stress, basin_velocity, basin_media)
        box_stress = grid_stress(box_stress, box_velocity, box_media)
    return basin_velocity, basin_stress, box_velocity, box_stress
```

```python
import functools

import jax
import jax.numpy as jnp
from jax import lax
from jax.experimental import pallas as pl
from jax.experimental.pallas import tpu as pltpu
from jax.sharding import PartitionSpec as P

NZ = 16
BZ = 8
CX = 64
CY = 128
ZR = 8
ZONES = 8
GROUPS = 64
BLK = 128
DT = 0.12
NEAR = 9.0 / 8.0
FAR = 1.0 / 24.0

VM = pl.BlockSpec(memory_space=pltpu.VMEM)
SM = pl.BlockSpec(memory_space=pltpu.SMEM)
PARAMS = pltpu.CompilerParams(vmem_limit_bytes=20 * 2**20)
F32 = jnp.float32
BF16 = jnp.bfloat16
XS = (0, 1, 2)
YS = (2, 3, 4)
VS = (0, 1, 2)


def sds(shape, dtype=F32):
    return jax.ShapeDtypeStruct(shape, dtype)


def lanes():
    return lax.broadcasted_iota(jnp.int32, (CX, CY), 1)


def slot(k0, layers, c):
    first = k0 + c * layers
    return first // 32, first % 32


def put_x(xlo_ref, xhi_ref, k, value):
    xlo_ref[k] = value[0:2]
    xhi_ref[k] = value[CX - 2 : CX]


def put_y(q_ref, j, m, value):
    moved = pltpu.roll(value, 2 + 4 * m, 1)
    q_ref[j] = jnp.where(lanes() // 4 == m, moved, q_ref[j])


def y_halo(qm_ref, j, m):
    return pltpu.roll(qm_ref[j], CY - 2 - 4 * m, 1)


def merge_q(flags_ref, ql_ref, qr_ref, qm_ref):
    part = lanes() % 4
    for j in range(ql_ref.shape[0]):
        left = jnp.where(flags_ref[2] > 0, ql_ref[j], 0.0)
        right = jnp.where(flags_ref[3] > 0, qr_ref[j], 0.0)
        qm_ref[j] = jnp.where(part < 2, left, right)


def fill_pad(flags_ref, src_ref, comps, xb_ref, xa_ref, k0, pad_ref, layers):
    def body(z, _):
        for i, c in enumerate(comps):
            k = k0 + i * layers + z
            pad_ref[i, z, 8 : 8 + CX] = src_ref[c, z]
            pad_ref[i, z, 6:8] = jnp.where(flags_ref[0] > 0, xb_ref[k], 0.0)
            pad_ref[i, z, 8 + CX : 10 + CX] = jnp.where(flags_ref[1] > 0, xa_ref[k], 0.0)
        return 0

    lax.fori_loop(0, layers, body, 0)


def dx(pad_ref, i, z, forward):
    def at(d):
        return pad_ref[i, z, 8 + d : 8 + d + CX]

    if forward:
        return NEAR * (at(1) - at(0)) - FAR * (at(2) - at(-1))
    return NEAR * (at(0) - at(-1)) - FAR * (at(1) - at(-2))


def dy(value, halo, forward):
    lane = lanes()
    before = pltpu.roll(jnp.where(lane >= CY - 1, halo, value), 1, 1)
    after = pltpu.roll(jnp.where(lane < 1, halo, value), CY - 1, 1)
    if forward:
        return NEAR * (after - value) - FAR * (pltpu.roll(jnp.where(lane < 2, halo, value), CY - 2, 1) - before)
    return NEAR * (value - before) - FAR * (after - pltpu.roll(jnp.where(lane >= CY - 2, halo, value), 2, 1))


def dz(src_ref, c, z, layers, forward, edge):
    def at(d):
        if edge and not 0 <= z + d < layers:
            return jnp.zeros((CX, CY), F32)
        return src_ref[c, z + d]

    if forward:
        return NEAR * (at(1) - at(0)) - FAR * (at(2) - at(-1))
    return NEAR * (at(0) - at(-1)) - FAR * (at(1) - at(-2))


def over_layers(layers, body):
    for z in (0, 1):
        body(z, True)

    def inner(z, _):
        body(z, False)
        return 0

    lax.fori_loop(2, layers - 2, inner, 0)
    for z in (layers - 2, layers - 1):
        body(z, True)


def pack_kernel(zm_ref, sb_ref, sx_ref, ids_ref, xlo_ref, xhi_ref, q_ref, med_ref):
    q_ref[...] = jnp.zeros(q_ref.shape, F32)
    for ref, layers, k0 in ((sb_ref, NZ, 0), (sx_ref, BZ, 3 * NZ)):

        def body(z, _, ref=ref, layers=layers, k0=k0):
            for i, c in enumerate(XS):
                put_x(xlo_ref, xhi_ref, k0 + i * layers + z, ref[c, z])
            for i, c in enumerate(YS):
                j, m = slot(k0, layers, i)
                put_y(q_ref, j, m + z, ref[c, z])
            return 0

        lax.fori_loop(0, layers, body, 0)

    def media(z, _):
        ids = ids_ref[z]
        for c in range(3):
            value = jnp.full((CX, CY), zm_ref[c, 0], F32)
            for n in range(1, ZONES):
                value = jnp.where(ids == n, zm_ref[c, n], value)
            med_ref[c, z] = value
        return 0

    lax.fori_loop(0, BZ, media, 0)


def start_edges(carried, xlo_ref, xhi_ref, q_ref):
    q_ref[...] = jnp.zeros(q_ref.shape, F32)
    if not carried:
        return 0
    done = carried[0].shape[0]
    xlo_ref[0:done] = carried[0][...]
    xhi_ref[0:done] = carried[1][...]
    q_ref[0 : carried[2].shape[0]] = carried[2][...]
    return done


def vel_kernel(layers, k0, forced, carry, *refs):
    flags_ref, v_ref, s_ref, med_ref, xb_ref, xa_ref, ql_ref, qr_ref = refs[:8]
    refs = refs[8:]
    if forced:
        force_ref, refs = refs[0], refs[1:]
    carried, refs = (refs[:3], refs[3:]) if carry else ((), refs)
    out_ref, xlo_ref, xhi_ref, q_ref, pad_ref, qm_ref = refs
    fill_pad(flags_ref, s_ref, XS, xb_ref, xa_ref, k0, pad_ref, layers)
    merge_q(flags_ref, ql_ref, qr_ref, qm_ref)
    o0 = start_edges(carried, xlo_ref, xhi_ref, q_ref)

    def body(z, edge):
        def ydiff(i, forward):
            j, m = slot(k0, layers, i)
            return dy(s_ref[YS[i], z], y_halo(qm_ref, j, m + z), forward)

        scale = DT * med_ref[2, z]
        sums = (
            dx(pad_ref, 0, z, True) + ydiff(0, False) + dz(s_ref, 1, z, layers, False, edge),
            dx(pad_ref, 2, z, False) + ydiff(2, True) + dz(s_ref, 3, z, layers, False, edge),
            dx(pad_ref, 1, z, False) + ydiff(1, False) + dz(s_ref, 5, z, layers, True, edge),
        )
        for c in VS:
            new = v_ref[c, z] + scale * sums[c]
            if forced and edge and z == layers - 1:
                new = new + scale * force_ref[c]
            out_ref[c, z] = new
            put_x(xlo_ref, xhi_ref, o0 + c * layers + z, new)
            j, m = slot(o0, layers, c)
            put_y(q_ref, j, m + z, new)

    over_layers(layers, body)


def stress_kernel(layers, k0, edges, *refs):
    flags_ref, v_ref, s_ref, med_ref, xb_ref, xa_ref, ql_ref, qr_ref, out_ref = refs[:9]
    refs = refs[9:]
    if edges:
        xlo_ref, xhi_ref, q_ref = refs[:3]
        refs = refs[3:]
        q_ref[...] = jnp.zeros(q_ref.shape, F32)
    pad_ref, qm_ref = refs
    fill_pad(flags_ref, v_ref, VS, xb_ref, xa_ref, k0, pad_ref, layers)
    merge_q(flags_ref, ql_ref, qr_ref, qm_ref)

    def body(z, edge):
        def halo(c):
            j, m = slot(k0, layers, c)
            return y_halo(qm_ref, j, m + z)

        lam, mu = DT * med_ref[0, z], DT * med_ref[1, z]
        mod = lam + 2.0 * mu
        hx, hy, hz = halo(0), halo(1), halo(2)
        ex = dx(pad_ref, 0, z, False)
        ey = dy(v_ref[1, z], hy, False)
        ez = dz(v_ref, 2, z, layers, False, edge)
        new = (
            s_ref[0, z] + (mod * ex + lam * (ey + ez)),
            s_ref[1, z] + mu * (dz(v_ref, 0, z, layers, True, edge) + dx(pad_ref, 2, z, True)),
            s_ref[2, z] + mu * (dy(v_ref[0, z], hx, True) + dx(pad_ref, 1, z, True)),
            s_ref[3, z] + mu * (dz(v_ref, 1, z, layers, True, edge) + dy(v_ref[2, z], hz, True)),
            s_ref[4, z] + (mod * ey + lam * (ex + ez)),
            s_ref[5, z] + (mod * ez + lam * (ex + ey)),
        )
        for c in range(6):
            out_ref[c, z] = new[c]
        if edges:
            for i, c in enumerate(XS):
                put_x(xlo_ref, xhi_ref, i * layers + z, new[c])
            for i, c in enumerate(YS):
                j, m = slot(0, layers, i)
                put_y(q_ref, j, m + z, new[c])

    over_layers(layers, body)


def row_lookup(idx_row):
    return jnp.broadcast_to(idx_row, (8, CY))


def take(table, index):
    return jnp.take_along_axis(table, index, axis=1, mode="promise_in_bounds")


def select_sorted(lo_ref, hi_ref, rs_ref, ys_ref, v_ref, sorted_ref):
    sub = lax.broadcasted_iota(jnp.int32, (8, CY), 0)
    top = v_ref.shape[0] * 8 - 1
    comps = v_ref.shape[1]
    several = 12 // comps

    def part(k, rows, index, accs):
        t, x = k // 8, pl.multiple_of(k % 8 * 8, 8)
        hit = rows == 8 * k
        return tuple(jnp.where(hit, take(v_ref[t, c, pl.ds(x, 8), :], index), accs[c]) for c in range(comps))

    def body(b, _):
        state = []
        for u in range(several):
            g = b * several + u
            index = row_lookup(ys_ref[pl.ds(g, 1), :])
            rows = row_lookup(rs_ref[pl.ds(g, 1), :]) - sub
            accs = (jnp.zeros((8, CY), F32),) * comps
            first = lo_ref[g]
            for d in range(2):
                accs = part(jnp.minimum(first + d, top), rows, index, accs)
            state.append((g, index, rows, first, accs))
        for g, index, rows, first, accs in state:
            accs = lax.fori_loop(
                first + 2, hi_ref[g] + 1, lambda k, a, r=rows, i=index: part(k, r, i, a), accs
            )
            for c in range(comps):
                sorted_ref[c, pl.ds(g, 1), :] = jnp.sum(accs[c], axis=0, keepdims=True)
        return 0

    lax.fori_loop(0, GROUPS // several, body, 0)


def unsort(sorted_ref, inv_ref, g):
    sub = lax.broadcasted_iota(jnp.int32, (8, CY), 0)
    place = row_lookup(inv_ref[pl.ds(g, 1), :])
    index = place & (CY - 1)
    rows = (place >> 7) - sub
    comps = sorted_ref.shape[0]
    accs = [jnp.zeros((8, CY), F32)] * comps
    for k in range(GROUPS // 8):
        hit = rows == 8 * k
        for c in range(comps):
            accs[c] = jnp.where(hit, take(sorted_ref[c, 8 * k : 8 * k + 8, :], index), accs[c])
    tiles = []
    for f in range(0, comps, 3):
        tile = jnp.zeros((8, CY), F32)
        for c in range(3):
            tile = jnp.where(sub == c, jnp.sum(accs[f + c], axis=0, keepdims=True), tile)
        tiles.append(tile)
    return tiles


def force_kernel(first, *refs):
    lo_ref, hi_ref, rs_ref, ys_ref, inv_ref, v_ref, stiff_ref, mass_ref = refs[:8]
    refs = refs[8:]
    if not first:
        prev_ref, refs = refs[0], refs[1:]
    force_ref, refs = refs[0], refs[1:]
    if first:
        cur_ref, refs = refs[0], refs[1:]
    (sorted_ref,) = refs
    select_sorted(lo_ref, hi_ref, rs_ref, ys_ref, v_ref, sorted_ref)
    several = 4

    def body(b, _):
        for u in range(several):
            g = b * several + u
            tiles = unsort(sorted_ref, inv_ref, g)
            tile = tiles[-1]
            if first:
                cur_ref[g] = tile
            change = (tile - (tiles[0] if first else prev_ref[g])) / DT
            both = jnp.concatenate([tile, change], axis=1)
            high = both.astype(BF16)
            low = (both - high.astype(F32)).astype(BF16)
            matrix = jnp.concatenate([stiff_ref[g], mass_ref[g]], axis=1)
            matrix_high = matrix.astype(BF16)
            matrix_low = (matrix - matrix_high.astype(F32)).astype(BF16)
            stacked = jnp.concatenate([high, low], axis=0)
            weights = jnp.concatenate([matrix_high, matrix_low], axis=0)
            product = lax.dot_general(stacked, weights, (((1,), (1,)), ((), ())), preferred_element_type=F32)
            total = product[0:8, 0:BLK] + (product[0:8, BLK:] + product[8:16, 0:BLK])
            for c in range(3):
                force_ref[c, pl.ds(g, 1), :] = -total[c : c + 1]
        return 0

    lax.fori_loop(0, GROUPS // several, body, 0)


def ring(value, axis, step):
    n = lax.axis_size(axis)
    return lax.ppermute(value, axis, [(i, (i + step) % n) for i in range(n)])


def trade(edges):
    xlo, xhi, q = edges
    return ring(xhi, "gx", 1), ring(xlo, "gx", -1), ring(q, "gy", 1), ring(q, "gy", -1)


def cost(flops, size):
    return pl.CostEstimate(flops=flops, bytes_accessed=size, transcendentals=0)


def edge_shapes(layers):
    k = 3 * layers
    return (sds((k, 2, CY)), sds((k, 2, CY)), sds((-(-k // 32), CX, CY)))


def velocity_step(name, flags, v, s, media, halos, k0, force=None, carry=()):
    layers = v.shape[1]
    out = pl.pallas_call(
        functools.partial(vel_kernel, layers, k0, force is not None, bool(carry)),
        out_shape=(sds(v.shape), *edge_shapes(layers + (carry[0].shape[0] // 3 if carry else 0))),
        in_specs=[SM] + [VM] * (7 + (force is not None) + len(carry)),
        out_specs=(VM,) * 4,
        scratch_shapes=[pltpu.VMEM((3, layers, CX + 16, CY), F32), pltpu.VMEM(halos[2].shape, F32)],
        compiler_params=PARAMS,
        name=name,
        cost_estimate=cost(60 * v.size, 16 * v.size),
    )(flags, v, s, media, *halos, *(() if force is None else (force,)), *carry)
    return out[0], out[1:]


def stress_step(name, flags, v, s, media, halos, k0, edges):
    layers = v.shape[1]
    out = pl.pallas_call(
        functools.partial(stress_kernel, layers, k0, edges),
        out_shape=(sds(s.shape), *(edge_shapes(layers) if edges else ())),
        in_specs=[SM] + [VM] * 7,
        out_specs=(VM,) * (4 if edges else 1),
        scratch_shapes=[pltpu.VMEM((3, layers, CX + 16, CY), F32), pltpu.VMEM(halos[2].shape, F32)],
        compiler_params=PARAMS,
        name=name,
        cost_estimate=cost(60 * v.size, 16 * v.size),
    )(flags, v, s, media, *halos)
    return out[0], out[1:]


def shards(
    basin_v, basin_s, basin_media, box_v, box_s, zone_ids, zone_media, corridor_tile, corridor_cell, drm_stiff, drm_mass
):
    gx, gy = lax.axis_index("gx"), lax.axis_index("gy")
    nx, ny = lax.axis_size("gx"), lax.axis_size("gy")
    flags = jnp.stack([gx > 0, gx < nx - 1, gy > 0, gy < ny - 1]).astype(jnp.int32)

    def spread(layer):
        return lax.all_to_all(jnp.broadcast_to(layer[None], (ny, *layer.shape)), "gy", 0, 0, tiled=True)

    *edges, box_media = pl.pallas_call(
        pack_kernel,
        out_shape=(*edge_shapes(NZ + BZ), sds((3, BZ, CX, CY))),
        in_specs=[SM, VM, VM, VM],
        out_specs=(VM,) * 4,
        compiler_params=PARAMS,
        name="pack",
        cost_estimate=cost(2**20, 2**22),
    )(zone_media, basin_s, box_s, zone_ids)
    halos = trade(edges)

    own_tile = lax.dynamic_index_in_dim(corridor_tile[0, :, :, 0], gy, 0, keepdims=False)
    own_cell = lax.dynamic_index_in_dim(corridor_cell[0], gy, 0, keepdims=False)
    requests = lax.iota(jnp.int32, GROUPS * BLK)
    keys = lax.sort((own_tile * (CX * CY) + own_cell) * (GROUPS * BLK) + requests)
    rows = (keys >> 20).reshape(GROUPS, BLK)
    cols = ((keys >> 13) & (CY - 1)).reshape(GROUPS, BLK)
    inverse = lax.sort(((keys & 8191) << 13) | requests)
    inverse = (inverse & 8191).reshape(GROUPS, BLK)
    first, last = rows[:, 0] >> 3, rows[:, BLK - 1] >> 3
    lookup = (first, last, rows, cols, inverse)

    def forces(name, layers, previous):
        first = previous is None
        comps = layers.shape[1]
        shapes = (sds((3, CX, CY)), sds((GROUPS, 8, BLK)))
        return pl.pallas_call(
            functools.partial(force_kernel, first),
            out_shape=shapes if first else shapes[:1],
            in_specs=[SM, SM] + [VM] * (6 if first else 7),
            out_specs=(VM, VM) if first else (VM,),
            scratch_shapes=[pltpu.VMEM((comps, GROUPS, BLK), F32)],
            compiler_params=PARAMS,
            name=name,
            cost_estimate=cost(2**30, 2**23),
        )(*lookup, layers, drm_stiff[0, 0], drm_mass[0, 0], *(() if first else (previous,)))

    layer0 = basin_v[:, ZR]
    basin_v, edges_b = velocity_step("basin_v1", flags, basin_v, basin_s, basin_media, halos, 0)
    layers01 = spread(jnp.concatenate([layer0, basin_v[:, ZR]]))
    halos_b = trade(edges_b)
    basin_s, edges_b = stress_step("basin_s1", flags, basin_v, basin_s, basin_media, halos_b, 0, True)
    force, current = forces("force1", layers01, None)
    box_v, edges = velocity_step("box_v1", flags, box_v, box_s, box_media, halos, 3 * NZ, force, edges_b)
    halos = trade(edges)
    basin_v, edges_b = velocity_step("basin_v2", flags, basin_v, basin_s, basin_media, halos, 0)
    layer2 = spread(basin_v[:, ZR])
    box_s, edges_x = stress_step("box_s1", flags, box_v, box_s, box_media, halos, 3 * NZ, True)
    halos_x = trade(edges_x)
    (force,) = forces("force2", layer2, current)
    box_v, edges = velocity_step("box_v2", flags, box_v, box_s, box_media, halos_x, 0, force, edges_b)
    halos = trade(edges)
    basin_s, _ = stress_step("basin_s2", flags, basin_v, basin_s, basin_media, halos, 0, False)
    box_s, _ = stress_step("box_s2", flags, box_v, box_s, box_media, halos, 3 * NZ, False)
    return basin_v, basin_s, box_v, box_s


def solution(mesh):
    field = P(None, None, "gx", "gy")
    return jax.shard_map(
        shards,
        mesh=mesh,
        in_specs=(
            field,
            field,
            field,
            field,
            field,
            P(None, "gx", "gy"),
            P(),
            P("gx", None, None, None),
            P("gx", None, None),
            P("gx", "gy", None, None, None),
            P("gx", "gy", None, None, None),
        ),
        out_specs=(field,) * 4,
        check_vma=False,
    )
```

```python
import functools

import jax
import jax.numpy as jnp
from jax import lax
from jax.experimental import pallas as pl
from jax.experimental.pallas import tpu as pltpu
from jax.sharding import PartitionSpec as P

NZ = 16
BZ = 8
CX = 64
CY = 128
ZR = 8
ZONES = 8
GROUPS = 64
BLK = 128
DT = 0.12
NEAR = 9.0 / 8.0
FAR = 1.0 / 24.0

VM = pl.BlockSpec(memory_space=pltpu.VMEM)
SM = pl.BlockSpec(memory_space=pltpu.SMEM)
HB = pl.BlockSpec(memory_space=pltpu.HBM)
PARAMS = pltpu.CompilerParams(vmem_limit_bytes=56 * 2**20)
F32 = jnp.float32
BF16 = jnp.bfloat16
XS = (0, 1, 2)
YS = (2, 3, 4)
VS = (0, 1, 2)


def sds(shape, dtype=F32):
    return jax.ShapeDtypeStruct(shape, dtype)


def lanes():
    return lax.broadcasted_iota(jnp.int32, (CX, CY), 1)


def slot(k0, layers, c):
    first = k0 + c * layers
    return first // 32, first % 32


def put_x(xlo_ref, xhi_ref, k, value):
    xlo_ref[k] = value[0:2]
    xhi_ref[k] = value[CX - 2 : CX]


def put_y(q_ref, j, m, value):
    moved = pltpu.roll(value, 2 + 4 * m, 1)
    q_ref[j] = jnp.where(lanes() // 4 == m, moved, q_ref[j])


def y_halo(qm_ref, j, m):
    return pltpu.roll(qm_ref[j], CY - 2 - 4 * m, 1)


def merge_q(flags_ref, ql_ref, qr_ref, qm_ref):
    part = lanes() % 4
    for j in range(ql_ref.shape[0]):
        left = jnp.where(flags_ref[2] > 0, ql_ref[j], 0.0)
        right = jnp.where(flags_ref[3] > 0, qr_ref[j], 0.0)
        qm_ref[j] = jnp.where(part < 2, left, right)


def fill_pad(flags_ref, src_ref, comps, xb_ref, xa_ref, k0, pad_ref, layers, group):
    def body(z, _):
        for i, c in enumerate(comps):
            k = k0 + i * layers + z
            pad_ref[i, z, 8 : 8 + CX] = src_ref[c, z]
            pad_ref[i, z, 6:8] = jnp.where(flags_ref[0] > 0, xb_ref[k], 0.0)
            pad_ref[i, z, 8 + CX : 10 + CX] = jnp.where(flags_ref[1] > 0, xa_ref[k], 0.0)
        return 0

    lax.fori_loop(*group, body, 0)


def dx(pad_ref, i, z, forward):
    def at(d):
        return pad_ref[i, z, 8 + d : 8 + d + CX]

    if forward:
        return NEAR * (at(1) - at(0)) - FAR * (at(2) - at(-1))
    return NEAR * (at(0) - at(-1)) - FAR * (at(1) - at(-2))


def fill_weights(w_ref):
    at = lax.broadcasted_iota(jnp.int32, (CY, CY), 0)
    to = lax.broadcasted_iota(jnp.int32, (CY, CY), 1)
    beyond = jnp.where(at >= CY - 2, at - CY, jnp.where(at < 2, at + CY, -CY))
    for forward in range(2):
        for part, source in enumerate((at, beyond)):
            offset = source - to - forward
            weight = jnp.where(offset == 0, 27.0, jnp.where(offset == -1, -27.0, 0.0))
            weight = jnp.where(offset == 1, -1.0, jnp.where(offset == -2, 1.0, weight)).astype(BF16)
            for copy in range(2):
                low = (2 * part + copy) * CY
                w_ref[forward, low : low + CY] = weight


def pieces(value):
    high = value.astype(BF16)
    return high, (value - high.astype(F32)).astype(BF16)


def fill_dy(group, src_ref, comps, forward, qm_ref, k0, layers, w_ref, t_ref, y_ref):
    a, b = group
    for i, c in enumerate(comps):
        j, m = slot(k0, layers, i)
        for z in range(a, b):
            low = (z - a) * CX
            terms = (*pieces(src_ref[c, z]), *pieces(y_halo(qm_ref, j, m + z)))
            for n, term in enumerate(terms):
                t_ref[i, low : low + CX, n * CY : (n + 1) * CY] = term
        result = jnp.dot(t_ref[i], w_ref[forward[i]], preferred_element_type=F32) * (1.0 / 24.0)
        for z in range(a, b):
            y_ref[i, z] = result[(z - a) * CX : (z - a + 1) * CX]


def dz(src_ref, c, z, layers, forward, edge):
    def at(d):
        if edge and not 0 <= z + d < layers:
            return jnp.zeros((CX, CY), F32)
        return src_ref[c, z + d]

    if forward:
        return NEAR * (at(1) - at(0)) - FAR * (at(2) - at(-1))
    return NEAR * (at(0) - at(-1)) - FAR * (at(1) - at(-2))


def over_layers(layers, group, body):
    low, high = max(group[0], 2), min(group[1], layers - 2)
    for z in range(group[0], low):
        body(z, True)

    def inner(z, _):
        body(z, False)
        return 0

    lax.fori_loop(low, high, inner, 0)
    for z in range(high, group[1]):
        body(z, True)


def groups_of(layers):
    return [(z, z + 4) for z in range(0, layers, 4)]


def streams(pairs, sem_ref, layers):
    return [
        [
            pltpu.make_async_copy(src.at[:, a:b], dst.at[:, a:b], sem_ref.at[p, n])
            for p, (src, dst) in enumerate(pairs)
        ]
        for n, (a, b) in enumerate(groups_of(layers))
    ]


def start_all(copies):
    for group in copies:
        for copy in group:
            copy.start()


def wait_group(copies, n):
    if n < len(copies):
        for copy in copies[n]:
            copy.wait()


def pack_kernel(zm_ref, sb_ref, sx_ref, ids_ref, xlo_ref, xhi_ref, q_ref, med_ref, b_ref, x_ref, b_sem, x_sem):
    copies_b = streams(((sb_ref.at[0:5], b_ref),), b_sem, NZ)
    copies_x = streams(((sx_ref.at[0:5], x_ref),), x_sem, BZ)
    start_all(copies_b)
    start_all(copies_x)
    q_ref[...] = jnp.zeros(q_ref.shape, F32)

    def media(z, _):
        ids = ids_ref[z]
        for c in range(3):
            value = jnp.full((CX, CY), zm_ref[c, 0], F32)
            for n in range(1, ZONES):
                value = jnp.where(ids == n, zm_ref[c, n], value)
            med_ref[c, z] = value
        return 0

    lax.fori_loop(0, BZ, media, 0)
    for ref, copies, layers, k0 in ((b_ref, copies_b, NZ, 0), (x_ref, copies_x, BZ, 3 * NZ)):

        def body(z, _, ref=ref, layers=layers, k0=k0):
            for i, c in enumerate(XS):
                put_x(xlo_ref, xhi_ref, k0 + i * layers + z, ref[c, z])
            for i, c in enumerate(YS):
                j, m = slot(k0, layers, i)
                put_y(q_ref, j, m + z, ref[c, z])
            return 0

        for n, group in enumerate(groups_of(layers)):
            wait_group(copies, n)
            lax.fori_loop(*group, body, 0)


def start_edges(carried, xlo_ref, xhi_ref, q_ref):
    q_ref[...] = jnp.zeros(q_ref.shape, F32)
    if not carried:
        return 0
    done = carried[0].shape[0]
    xlo_ref[0:done] = carried[0][...]
    xhi_ref[0:done] = carried[1][...]
    q_ref[0 : carried[2].shape[0]] = carried[2][...]
    return done


def sweep(layers, copies, results, body, prepare, finish=True):
    wait_group(copies, 0)
    for n, group in enumerate(groups_of(layers)):
        wait_group(copies, n + 1)
        prepare(group)
        over_layers(layers, group, body)
        for result in results[n]:
            result.start()
    for n in range(len(results) if finish else 0):
        wait_group(results, n)


def vel_kernel(layers, k0, forced, carry, *refs, before=None, sent=0):
    flags_ref, v_ref, s_ref, med_ref, xb_ref, xa_ref, ql_ref, qr_ref = refs[:8]
    refs = refs[8:]
    if forced:
        force_ref, refs = refs[0], refs[1:]
    carried, refs = (refs[:3], refs[3:]) if carry else ((), refs)
    hbm_v, hbm_s, hbm_med = v_ref, s_ref, med_ref
    hbm_out, xlo_ref, xhi_ref, q_ref = refs[:4]
    refs = refs[4:]
    if sent:
        hbm_sent, refs = refs[0], refs[1:]
    pad_ref, qm_ref, w_ref, t_ref, y_ref, v_ref, s_ref, med_ref, out_ref, in_sem, out_sem, *sent_sem = refs
    copies = streams(((hbm_s, s_ref), (hbm_v, v_ref), (hbm_med.at[2:3], med_ref)), in_sem, layers)
    results = streams(((out_ref, hbm_out),), out_sem, layers)
    for t in range(hbm_sent.shape[0] if sent else 0):
        results[ZR // 4].append(pltpu.make_async_copy(out_ref.at[:, ZR], hbm_sent.at[t, sent - 3 : sent], sent_sem[0].at[1, t]))
        if sent == 6:
            results[ZR // 4].append(pltpu.make_async_copy(v_ref.at[:, ZR], hbm_sent.at[t, 0:3], sent_sem[0].at[0, t]))
    start_all(copies)
    fill_weights(w_ref)
    merge_q(flags_ref, ql_ref, qr_ref, qm_ref)
    o0 = start_edges(carried, xlo_ref, xhi_ref, q_ref)
    if before:
        before()

    def body(z, edge):
        scale = DT * med_ref[0, z]
        sums = (
            dx(pad_ref, 0, z, True) + y_ref[0, z] + dz(s_ref, 1, z, layers, False, edge),
            dx(pad_ref, 2, z, False) + y_ref[2, z] + dz(s_ref, 3, z, layers, False, edge),
            dx(pad_ref, 1, z, False) + y_ref[1, z] + dz(s_ref, 5, z, layers, True, edge),
        )
        for c in VS:
            new = v_ref[c, z] + scale * sums[c]
            if forced and edge and z == layers - 1:
                new = new + scale * force_ref[c]
            out_ref[c, z] = new
            put_x(xlo_ref, xhi_ref, o0 + c * layers + z, new)
            j, m = slot(o0, layers, c)
            put_y(q_ref, j, m + z, new)

    def prepare(group):
        fill_pad(flags_ref, s_ref, XS, xb_ref, xa_ref, k0, pad_ref, layers, group)
        fill_dy(group, s_ref, YS, (0, 0, 1), qm_ref, k0, layers, w_ref, t_ref, y_ref)

    sweep(layers, copies, results, body, prepare)


def stress_parts(layers, k0, edges, *refs):
    flags_ref, hbm_v, hbm_s, hbm_med, xb_ref, xa_ref, ql_ref, qr_ref, hbm_out = refs[:9]
    refs = refs[9:]
    if edges:
        xlo_ref, xhi_ref, q_ref = refs[:3]
        refs = refs[3:]
        q_ref[...] = jnp.zeros(q_ref.shape, F32)
    pad_ref, qm_ref, w_ref, t_ref, y_ref, v_ref, s_ref, med_ref, out_ref, in_sem, out_sem = refs
    copies = streams(((hbm_v, v_ref), (hbm_s, s_ref), (hbm_med.at[0:2], med_ref)), in_sem, layers)
    results = streams(((out_ref, hbm_out),), out_sem, layers)
    start_all(copies)
    fill_weights(w_ref)
    merge_q(flags_ref, ql_ref, qr_ref, qm_ref)

    def body(z, edge):
        lam, mu = DT * med_ref[0, z], DT * med_ref[1, z]
        mod = lam + 2.0 * mu
        ex = dx(pad_ref, 0, z, False)
        ey = y_ref[1, z]
        ez = dz(v_ref, 2, z, layers, False, edge)
        new = (
            s_ref[0, z] + (mod * ex + lam * (ey + ez)),
            s_ref[1, z] + mu * (dz(v_ref, 0, z, layers, True, edge) + dx(pad_ref, 2, z, True)),
            s_ref[2, z] + mu * (y_ref[0, z] + dx(pad_ref, 1, z, True)),
            s_ref[3, z] + mu * (dz(v_ref, 1, z, layers, True, edge) + y_ref[2, z]),
            s_ref[4, z] + (mod * ey + lam * (ex + ez)),
            s_ref[5, z] + (mod * ez + lam * (ex + ey)),
        )
        for c in range(6):
            out_ref[c, z] = new[c]
        if edges:
            for i, c in enumerate(XS):
                put_x(xlo_ref, xhi_ref, i * layers + z, new[c])
            for i, c in enumerate(YS):
                j, m = slot(0, layers, i)
                put_y(q_ref, j, m + z, new[c])

    def prepare(group):
        fill_pad(flags_ref, v_ref, VS, xb_ref, xa_ref, k0, pad_ref, layers, group)
        fill_dy(group, v_ref, VS, (1, 0, 1), qm_ref, k0, layers, w_ref, t_ref, y_ref)

    return (layers, copies, results, body, prepare), results


def stress_kernel(layers, k0, edges, *refs):
    arguments, _ = stress_parts(layers, k0, edges, *refs)
    sweep(*arguments)


def stress_pair_kernel(flags_ref, *refs):
    basin, box, halos, (out_b, out_x), refs = refs[0:3], refs[3:6], refs[6:10], refs[10:12], refs[12:]
    half = len(refs) // 2
    basin, results_b = stress_parts(NZ, 0, False, flags_ref, *basin, *halos, out_b, *refs[:half])
    box, results_x = stress_parts(BZ, 3 * NZ, False, flags_ref, *box, *halos, out_x, *refs[half:])
    sweep(*basin, finish=False)
    sweep(*box, finish=False)
    for results in (results_b, results_x):
        for n in range(len(results)):
            wait_group(results, n)


def forced_velocity_kernel(first, layers, k0, *refs):
    n = 8 if first else 9
    force_in, vel_in, refs = refs[:n], refs[n : n + 11], refs[n + 11 :]
    vel_out, refs = refs[:4], refs[4:]
    current, refs = (refs[:1], refs[1:]) if first else ((), refs)
    force_ref, force_scratch, vel_scratch = refs[0], refs[1:5], refs[5:]
    vel_kernel(
        layers,
        k0,
        True,
        True,
        *vel_in[:8],
        force_ref,
        *vel_in[8:],
        *vel_out,
        *vel_scratch,
        before=lambda: force_kernel(first, *force_in, force_ref, *current, *force_scratch),
    )


def row_lookup(idx_row):
    return jnp.broadcast_to(idx_row, (8, CY))


def take(table, index):
    return jnp.take_along_axis(table, index, axis=1, mode="promise_in_bounds")


def select_sorted(lo_ref, hi_ref, rs_ref, ys_ref, v_ref, sorted_ref):
    sub = lax.broadcasted_iota(jnp.int32, (8, CY), 0)
    top = v_ref.shape[0] * 8 - 1
    comps = v_ref.shape[1]
    several = 12 // comps

    def part(k, rows, index, accs):
        t, x = k // 8, pl.multiple_of(k % 8 * 8, 8)
        hit = rows == 8 * k
        return tuple(jnp.where(hit, take(v_ref[t, c, pl.ds(x, 8), :], index), accs[c]) for c in range(comps))

    def body(b, _):
        state = []
        for u in range(several):
            g = b * several + u
            index = row_lookup(ys_ref[pl.ds(g, 1), :])
            rows = row_lookup(rs_ref[pl.ds(g, 1), :]) - sub
            accs = (jnp.zeros((8, CY), F32),) * comps
            first = lo_ref[g]
            for d in range(2):
                accs = part(jnp.minimum(first + d, top), rows, index, accs)
            state.append((g, index, rows, first, accs))
        for g, index, rows, first, accs in state:
            accs = lax.fori_loop(
                first + 2, hi_ref[g] + 1, lambda k, a, r=rows, i=index: part(k, r, i, a), accs
            )
            for c in range(comps):
                sorted_ref[c, pl.ds(g, 1), :] = jnp.sum(accs[c], axis=0, keepdims=True)
        return 0

    lax.fori_loop(0, GROUPS // several, body, 0)


def unsort(sorted_ref, inv_ref, g):
    sub = lax.broadcasted_iota(jnp.int32, (8, CY), 0)
    place = row_lookup(inv_ref[pl.ds(g, 1), :])
    index = place & (CY - 1)
    rows = (place >> 7) - sub
    comps = sorted_ref.shape[0]
    accs = [jnp.zeros((8, CY), F32)] * comps
    for k in range(GROUPS // 8):
        hit = rows == 8 * k
        for c in range(comps):
            accs[c] = jnp.where(hit, take(sorted_ref[c, 8 * k : 8 * k + 8, :], index), accs[c])
    tiles = []
    for f in range(0, comps, 3):
        tile = jnp.zeros((8, CY), F32)
        for c in range(3):
            tile = jnp.where(sub == c, jnp.sum(accs[f + c], axis=0, keepdims=True), tile)
        tiles.append(tile)
    return tiles


def inverse_kernel(keys_ref, inv_ref):
    row = lax.broadcasted_iota(jnp.int32, (GROUPS, BLK), 0)
    column = lax.broadcasted_iota(jnp.int32, (BLK, BLK), 0)
    lane = lax.broadcasted_iota(jnp.int32, (GROUPS, BLK), 1).astype(F32)

    def body(b, total):
        parts, hots = [], []
        for u in range(8):
            g = b * 8 + u
            place = keys_ref[pl.ds(g, 1), :] & (GROUPS * BLK - 1)
            hit = row == (place >> 7)
            where_to = jnp.where(hit, lane, 0.0)
            parts.append(jnp.concatenate([where_to, jnp.where(hit, g.astype(F32), 0.0)], axis=0).astype(BF16))
            hots.append(jnp.where(column == (place & (BLK - 1)), 1.0, 0.0).astype(BF16))
        return total + lax.dot_general(
            jnp.concatenate(parts, axis=1),
            jnp.concatenate(hots, axis=1),
            (((1,), (1,)), ((), ())),
            preferred_element_type=F32,
        )

    total = lax.fori_loop(0, GROUPS // 8, body, jnp.zeros((2 * GROUPS, BLK), F32))
    inv_ref[...] = (total[0:GROUPS] + total[GROUPS:] * BLK).astype(jnp.int32)


def force_kernel(first, *refs):
    lo_ref, hi_ref, rs_ref, ys_ref, inv_ref, v_ref, hbm_stiff, hbm_mass = refs[:8]
    refs = refs[8:]
    if not first:
        prev_ref, refs = refs[0], refs[1:]
    force_ref, refs = refs[0], refs[1:]
    if first:
        cur_ref, refs = refs[0], refs[1:]
    sorted_ref, stiff_ref, mass_ref, sem_ref = refs
    several = 8

    def matrices(b):
        part = pl.ds(b * several, several)
        return [
            pltpu.make_async_copy(src.at[part], dst.at[part], sem_ref.at[i, b])
            for i, (src, dst) in enumerate(((hbm_stiff, stiff_ref), (hbm_mass, mass_ref)))
        ]

    def fetch(b, _):
        for copy in matrices(b):
            copy.start()
        return 0

    lax.fori_loop(0, GROUPS // several, fetch, 0)
    select_sorted(lo_ref, hi_ref, rs_ref, ys_ref, v_ref, sorted_ref)

    def body(b, _):
        for copy in matrices(b):
            copy.wait()
        for u in range(several):
            g = b * several + u
            tiles = unsort(sorted_ref, inv_ref, g)
            tile = tiles[-1]
            if first:
                cur_ref[g] = tile
            change = (tile - (tiles[0] if first else prev_ref[g])) / DT
            both = jnp.concatenate([tile, change], axis=1)
            high = both.astype(BF16)
            low = (both - high.astype(F32)).astype(BF16)
            matrix = jnp.concatenate([stiff_ref[g], mass_ref[g]], axis=1)
            matrix_high = matrix.astype(BF16)
            matrix_low = (matrix - matrix_high.astype(F32)).astype(BF16)
            stacked = jnp.concatenate([high, low], axis=0)
            weights = jnp.concatenate([matrix_high, matrix_low], axis=0)
            product = lax.dot_general(stacked, weights, (((1,), (1,)), ((), ())), preferred_element_type=F32)
            total = product[0:8, 0:BLK] + (product[0:8, BLK:] + product[8:16, 0:BLK])
            for c in range(3):
                force_ref[c, pl.ds(g, 1), :] = -total[c : c + 1]
        return 0

    lax.fori_loop(0, GROUPS // several, body, 0)


def ring(value, axis, step):
    n = lax.axis_size(axis)
    return lax.ppermute(value, axis, [(i, (i + step) % n) for i in range(n)])


def trade(edges):
    xlo, xhi, q = edges
    return ring(xhi, "gx", 1), ring(xlo, "gx", -1), ring(q, "gy", 1), ring(q, "gy", -1)


def cost(flops, size):
    return pl.CostEstimate(flops=flops, bytes_accessed=size, transcendentals=0)


def edge_shapes(layers):
    k = 3 * layers
    return (sds((k, 2, CY)), sds((k, 2, CY)), sds((-(-k // 32), CX, CY)))


def scratch(layers, q_shape, medias, results):
    n = len(groups_of(layers))
    return [
        pltpu.VMEM((3, layers, CX + 16, CY), F32),
        pltpu.VMEM(q_shape, F32),
        pltpu.VMEM((2, 4 * CY, CY), BF16),
        pltpu.VMEM((3, 4 * CX, 4 * CY), BF16),
        pltpu.VMEM((3, layers, CX, CY), F32),
        *(pltpu.VMEM((c, layers, CX, CY), F32) for c in (3, 6, medias, results)),
        pltpu.SemaphoreType.DMA((3, n)),
        pltpu.SemaphoreType.DMA((1, n)),
    ]


def velocity_step(name, flags, v, s, media, halos, k0, tiles, sent):
    layers = v.shape[1]
    out = pl.pallas_call(
        functools.partial(vel_kernel, layers, k0, False, False, sent=sent),
        out_shape=(sds(v.shape), *edge_shapes(layers), sds((tiles, sent, CX, CY))),
        in_specs=[SM] + [HB] * 3 + [VM] * 4,
        out_specs=(HB, VM, VM, VM, HB),
        scratch_shapes=[*scratch(layers, halos[2].shape, 1, 3), pltpu.SemaphoreType.DMA((2, tiles))],
        compiler_params=PARAMS,
        name=name,
        cost_estimate=cost(60 * v.size, 16 * v.size),
    )(flags, v, s, media, *halos)
    return out[0], out[1:4], out[4]


def stress_step(name, flags, v, s, media, halos, k0, edges):
    layers = v.shape[1]
    out = pl.pallas_call(
        functools.partial(stress_kernel, layers, k0, edges),
        out_shape=(sds(s.shape), *(edge_shapes(layers) if edges else ())),
        in_specs=[SM] + [HB] * 3 + [VM] * 4,
        out_specs=(HB, VM, VM, VM) if edges else (HB,),
        scratch_shapes=scratch(layers, halos[2].shape, 2, 6),
        compiler_params=PARAMS,
        name=name,
        cost_estimate=cost(60 * v.size, 16 * v.size),
    )(flags, v, s, media, *halos)
    return out[0], out[1:]


def shards(
    basin_v, basin_s, basin_media, box_v, box_s, zone_ids, zone_media, corridor_tile, corridor_cell, drm_stiff, drm_mass
):
    gx, gy = lax.axis_index("gx"), lax.axis_index("gy")
    nx, ny = lax.axis_size("gx"), lax.axis_size("gy")
    flags = jnp.stack([gx > 0, gx < nx - 1, gy > 0, gy < ny - 1]).astype(jnp.int32)

    def spread(layer):
        return lax.all_to_all(layer, "gy", 0, 0, tiled=True)

    *edges, box_media = pl.pallas_call(
        pack_kernel,
        out_shape=(*edge_shapes(NZ + BZ), sds((3, BZ, CX, CY))),
        in_specs=[SM, HB, HB, VM],
        out_specs=(VM,) * 4,
        scratch_shapes=[
            pltpu.VMEM((5, NZ, CX, CY), F32),
            pltpu.VMEM((5, BZ, CX, CY), F32),
            pltpu.SemaphoreType.DMA((1, NZ // 4)),
            pltpu.SemaphoreType.DMA((1, BZ // 4)),
        ],
        compiler_params=PARAMS,
        name="pack",
        cost_estimate=cost(2**20, 2**22),
    )(zone_media, basin_s, box_s, zone_ids)
    halos = trade(edges)

    own_tile = lax.dynamic_index_in_dim(corridor_tile[0, :, :, 0], gy, 0, keepdims=False)
    own_cell = lax.dynamic_index_in_dim(corridor_cell[0], gy, 0, keepdims=False)
    requests = lax.iota(jnp.int32, GROUPS * BLK)
    keys = lax.sort((own_tile * (CX * CY) + own_cell) * (GROUPS * BLK) + requests)
    rows = (keys >> 20).reshape(GROUPS, BLK)
    cols = ((keys >> 13) & (CY - 1)).reshape(GROUPS, BLK)
    inverse = pl.pallas_call(
        inverse_kernel,
        out_shape=sds((GROUPS, BLK), jnp.int32),
        in_specs=[VM],
        out_specs=VM,
        compiler_params=PARAMS,
        name="inverse",
        cost_estimate=cost(2**27, 2**16),
    )(keys.reshape(GROUPS, BLK))
    first, last = rows[:, 0] >> 3, rows[:, BLK - 1] >> 3
    lookup = (first, last, rows, cols, inverse)

    def forced_velocity(name, layers, previous, v, s, media, halos, k0, carry):
        first = previous is None
        depth = v.shape[1]
        shapes = (sds(v.shape), *edge_shapes(depth + carry[0].shape[0] // 3), sds((GROUPS, 8, BLK)))
        return pl.pallas_call(
            functools.partial(forced_velocity_kernel, first, depth, k0),
            out_shape=shapes if first else shapes[:4],
            in_specs=[SM, SM] + [VM] * 4 + [HB] * 2 + [VM] * (not first) + [SM] + [HB] * 3 + [VM] * 7,
            out_specs=(HB, VM, VM, VM, VM) if first else (HB, VM, VM, VM),
            scratch_shapes=[
                pltpu.VMEM((3, CX, CY), F32),
                pltpu.VMEM((layers.shape[1], GROUPS, BLK), F32),
                pltpu.VMEM((GROUPS, BLK, BLK), F32),
                pltpu.VMEM((GROUPS, BLK, BLK), F32),
                pltpu.SemaphoreType.DMA((2, GROUPS // 8)),
                *scratch(depth, halos[2].shape, 1, 3),
            ],
            compiler_params=PARAMS,
            name=name,
            cost_estimate=cost(2**30, 2**24),
        )(
            *lookup,
            layers,
            drm_stiff[0, 0],
            drm_mass[0, 0],
            *(() if first else (previous,)),
            flags,
            v,
            s,
            media,
            *halos,
            *carry,
        )

    basin_v, edges_b, layers01 = velocity_step(
        "basin_v1", flags, basin_v, basin_s, basin_media, halos, 0, ny, 6
    )
    layers01 = spread(layers01)
    halos_b = trade(edges_b)
    basin_s, edges_b = stress_step("basin_s1", flags, basin_v, basin_s, basin_media, halos_b, 0, True)
    box_v, *edges, current = forced_velocity(
        "box_v1", layers01, None, box_v, box_s, box_media, halos, 3 * NZ, edges_b
    )
    halos = trade(edges)
    basin_v, edges_b, layer2 = velocity_step("basin_v2", flags, basin_v, basin_s, basin_media, halos, 0, ny, 3)
    layer2 = spread(layer2)
    box_s, edges_x = stress_step("box_s1", flags, box_v, box_s, box_media, halos, 3 * NZ, True)
    halos_x = trade(edges_x)
    box_v, *edges = forced_velocity("box_v2", layer2, current, box_v, box_s, box_media, halos_x, 0, edges_b)
    halos = trade(edges)
    basin_s, box_s = pl.pallas_call(
        stress_pair_kernel,
        out_shape=(sds(basin_s.shape), sds(box_s.shape)),
        in_specs=[SM] + [HB] * 6 + [VM] * 4,
        out_specs=(HB, HB),
        scratch_shapes=[*scratch(NZ, halos[2].shape, 2, 6), *scratch(BZ, halos[2].shape, 2, 6)],
        compiler_params=PARAMS,
        name="stress2",
        cost_estimate=cost(2**26, 2**24),
    )(flags, basin_v, basin_s, basin_media, box_v, box_s, box_media, *halos)
    return basin_v, basin_s, box_v, box_s


def solution(mesh):
    field = P(None, None, "gx", "gy")
    return jax.shard_map(
        shards,
        mesh=mesh,
        in_specs=(
            field,
            field,
            field,
            field,
            field,
            P(None, "gx", "gy"),
            P(),
            P("gx", None, None, None),
            P("gx", None, None),
            P("gx", "gy", None, None, None),
            P("gx", "gy", None, None, None),
        ),
        out_specs=(field,) * 4,
        check_vma=False,
    )
```
